32 devices in a mesh: leaf: 8 (over z, x), sib: 4 (over y, core).
Axes of the slice: x: 2, y: 2, z: 4, core: 2. Of those that a mesh axis runs over, the one named last changes fastest.
Arguments:
- sources: float32 [16384, 128], P(('leaf', 'sib')), may hold values from -8 to 8
- ordering: int32 [16384], P(('leaf', 'sib')), may hold values from 0 to 16383, as said below
- diagonal_inverse: float32 [64, 256, 256], P(('leaf', 'sib')), as said below
- low_rank: float32 [16384, 128], P(('leaf', 'sib'))
- nearby_blocks: bfloat16 [64, 8, 256, 256], P(('leaf', 'sib')), may hold values from -0.125 to 0.125
- near_index: int32 [64, 8], P(('leaf', 'sib')), may hold values from 0 to 63, as said below
Outputs:
- solution: float32 [16384, 128], P(('leaf', 'sib'))
- coefficients: float32 [128, 128], replicated
The draws below stay inside these ranges and needn't reach their ends.
Inputs may be any that keep to these rules, and one draw needn't show every extreme that they name: `ordering`: each catalog row appears once, and the rows of leaf block i are i * 256 to i * 256 + 255. `near_index`: each entry names a leaf block other than its row's own, at most 2 blocks away from it; the distance 2 occurs. `diagonal_inverse`: each block is symmetric positive definite.
All inputs are finite; a program needn't handle non-finite values.
Results may differ from the reference program's by a relative error of at most 0.0034.
Values may be sent and summed in bfloat16 or wider, within the bound.
A program may use at most 64 MiB of HBM per device.

```python
import math
import jax
import jax.numpy as jnp
from jax import lax

LEAF = 256
RHS = 128
FACTOR_RANK = 128
NEAR = 8
ITERS = 4
LEAF_DEV = 2
LEAVES = 64
POINTS = 16384


def ordering_values(key):
    keys = jax.random.split(key, LEAVES)
    shuffled = jax.vmap(lambda single: jax.random.permutation(single, LEAF))(keys)
    offsets = jnp.arange(LEAVES, dtype=jnp.int32)[:, None] * LEAF
    return (shuffled.astype(jnp.int32) + offsets).reshape(-1).astype(jnp.int32)


def factor_values(key):
    first_key, second_key = jax.random.split(jax.random.fold_in(key, 13), 2)
    position = jnp.arange(POINTS, dtype=jnp.float32) / POINTS
    profile = 1.0 + 2.0 * position
    rough = jnp.exp(jax.random.uniform(first_key, (POINTS,), jnp.float32, 0.0, math.log(10.0)))
    base = jax.random.normal(second_key, (POINTS, FACTOR_RANK), jnp.float32)
    scale = 0.15 / math.sqrt(POINTS)
    return (base * (profile * rough)[:, None] * scale).astype(jnp.float32)


def draw_ordering(key, part):
    return ordering_values(key)


def draw_low_rank(key, part):
    return factor_values(key)


def draw_sources(key, part):
    sign_key, noise_key = jax.random.split(jax.random.fold_in(key, 17))
    factor = factor_values(key)
    leaf_order = ordering_values(key)
    column_ids = jnp.arange(RHS, dtype=jnp.int32) % FACTOR_RANK
    shifted_ids = (jnp.arange(RHS, dtype=jnp.int32) + 3) % FACTOR_RANK
    signs = jax.random.randint(sign_key, (2, RHS), 0, 2).astype(jnp.float32) * 2.0 - 1.0
    flow = factor[:, column_ids] * signs[0][None, :] + 0.5 * factor[:, shifted_ids] * signs[1][None, :]
    flow = flow * (0.3 * math.sqrt(POINTS))
    catalog = jnp.zeros((POINTS, RHS), jnp.float32).at[leaf_order].set(flow)
    noise = jax.random.normal(noise_key, (POINTS, RHS), jnp.float32)
    return jnp.clip(catalog + noise, -8.0, 8.0).astype(jnp.float32)


def draw_near_index(key, part):
    first_key, second_key = jax.random.split(jax.random.fold_in(key, 7))
    distance = jax.random.randint(first_key, (LEAVES, NEAR), 1, LEAF_DEV + 1)
    direction = jax.random.randint(second_key, (LEAVES, NEAR), 0, 2) * 2 - 1
    row_ids = jnp.arange(LEAVES, dtype=jnp.int32)[:, None]
    target = row_ids + direction * distance
    outside = (target < 0) | (target >= LEAVES)
    target = jnp.where(outside, row_ids - direction * distance, target)
    target = target.at[0, 0].set(LEAF_DEV)
    return target.astype(jnp.int32)


def draw_diagonal_inverse(key, part):
    first_key, second_key = jax.random.split(jax.random.fold_in(key, 11))
    diagonal = jax.random.uniform(first_key, (LEAVES, LEAF), jnp.float32, 0.6, 1.0)
    noise = jax.random.normal(second_key, (LEAVES, LEAF, LEAF), jnp.float32)
    symmetric = (noise + jnp.swapaxes(noise, 1, 2)) * (0.12 / math.sqrt(LEAF))
    identity = jnp.eye(LEAF, dtype=jnp.float32)
    return (symmetric + identity[None, :, :] * diagonal[:, :, None]).astype(jnp.float32)


def block_scale(key, shape, cuts, smallest, top_value):
    factor_of = 1.0
    for dim, parts in cuts:
        draws = jax.random.uniform(jax.random.fold_in(jax.random.fold_in(key, 6), dim), (parts,), jnp.float32, smallest / len(cuts), top_value / len(cuts))
        factor_of = factor_of * jnp.repeat(jnp.exp(draws), shape[dim] // parts).reshape((-1,) + (1,) * (len(shape) - 1 - dim))
    return factor_of


def bell_draw(stream_key, extent, deviation, reach, shards=(), held_as=jnp.bfloat16):
    result = deviation * jax.random.normal(stream_key, extent, jnp.float32)
    if shards:
        result = result * block_scale(stream_key, extent, shards, -0.22, 0.18)
    return jnp.clip(result, -reach, reach).astype(held_as)


def setup_inputs(seed: int = 0) -> dict:
    seeds = jax.random.split(jax.random.key(seed), 7)
    sources = draw_sources(jax.random.fold_in(seeds[6], 71), 0)
    ordering = draw_ordering(jax.random.fold_in(seeds[6], 71), 0)
    diagonal_inverse = draw_diagonal_inverse(jax.random.fold_in(seeds[6], 71), 0)
    low_rank = draw_low_rank(jax.random.fold_in(seeds[6], 71), 0)
    nearby_blocks = bell_draw(seeds[4], (LEAVES, NEAR, LEAF, LEAF), (LEAF * NEAR) ** -0.5, 0.125, ((0, 32),))
    near_index = draw_near_index(jax.random.fold_in(seeds[6], 71), 0)
    return dict(sources=sources, ordering=ordering, diagonal_inverse=diagonal_inverse, low_rank=low_rank, nearby_blocks=nearby_blocks, near_index=near_index)


def reference(sources, ordering, diagonal_inverse, low_rank, nearby_blocks, near_index):
    highest_setting = lax.Precision.HIGHEST
    leaves = diagonal_inverse.shape[0]
    ordered_rows = sources[ordering].reshape(leaves, LEAF, RHS)
    block_list = low_rank.reshape(leaves, LEAF, FACTOR_RANK)
    lifted_vector = jnp.einsum('zym,zmw->zyw', diagonal_inverse, block_list, precision=highest_setting)
    core_matrix = jnp.eye(FACTOR_RANK, dtype=jnp.float32) + jnp.einsum('wju,wjp->up', block_list, lifted_vector, precision=highest_setting)
    triangle = jnp.linalg.cholesky(core_matrix)

    def apply_inverse(input_vector):
        scaled_rows = jnp.einsum('zym,zmw->zyw', diagonal_inverse, input_vector, precision=highest_setting)
        projected_rows = jnp.einsum('wju,wjp->up', block_list, scaled_rows, precision=highest_setting)
        coefficients = jax.scipy.linalg.cho_solve((triangle, True), projected_rows)
        result_vector = scaled_rows - jnp.einsum('eqb,bd->eqd', lifted_vector, coefficients, precision=highest_setting)
        return (result_vector, coefficients)
    iterate, coefficients = apply_inverse(ordered_rows)
    for sweep in range(ITERS):
        rounded = iterate.astype(jnp.bfloat16)

        def near_row(leaf_row):
            targets = near_index[leaf_row]
            piece_list = rounded[targets].astype(jnp.float32)
            return jnp.einsum('kab,kbr->ar', nearby_blocks[leaf_row].astype(jnp.float32), piece_list)
        image_vector = lax.map(near_row, jnp.arange(leaves, dtype=jnp.int32))
        iterate, coefficients = apply_inverse(ordered_rows - image_vector)
    return (iterate.reshape(leaves * LEAF, RHS), coefficients)
```

```python
import functools

import jax
import jax.numpy as jnp
from jax import lax
from jax.experimental import pallas as pl
from jax.experimental.pallas import tpu as pltpu
from jax.sharding import PartitionSpec as P

ITERS = 4
MESH = pl.DeviceIdType.MESH
HIGH = lax.Precision.HIGHEST
SUMS = (2, ITERS - 1) + (1,) * ITERS
PIVOTS = 8


def mm(a, b):
    return jnp.dot(a, b, precision=HIGH, preferred_element_type=jnp.float32)


def mm_t(a, b):
    return lax.dot_general(
        a, b, (((0,), (0,)), ((), ())), precision=HIGH, preferred_element_type=jnp.float32
    )


def invert(work):
    size = work.shape[0]
    lane = lax.broadcasted_iota(jnp.int32, (PIVOTS, size), 1)
    sub = lax.broadcasted_iota(jnp.int32, (PIVOTS, size), 0)
    wide = lax.broadcasted_iota(jnp.int32, (size, size), 1)
    for off in range(0, size, PIVOTS):
        panel = work[off : off + PIVOTS, :]
        left = jnp.where(lane < off, -panel, panel)
        for j in range(PIVOTS):
            c = off + j
            inv = 1.0 / panel[j : j + 1, c : c + 1]
            row = jnp.where(lane == c, inv, panel[j : j + 1, :] * inv)
            rest = jnp.where(lane == c, 0.0, panel) - panel[:, c : c + 1] * row
            panel = jnp.where(sub == j, row, rest)
        inside = (wide >= off) & (wide < off + PIVOTS)
        work[...] = jnp.where(inside, 0.0, work[...]) - mm_t(left, panel)
        work[off : off + PIVOTS, :] = panel


class Sum:
    def __init__(self, me, sizes, refs):
        self.leaf, self.sib = me
        self.n_leaf, self.n_sib = sizes
        self.src, self.r1, self.r2, self.r3, *self.sems = refs
        self.chunk = self.r1.shape[1]
        self.open = []

    def copy(self, src, dst, phase, o, target):
        send, recv = self.sems[2 * phase], self.sems[2 * phase + 1]
        c = pltpu.make_async_remote_copy(
            src_ref=src, dst_ref=dst, send_sem=send.at[o], recv_sem=recv.at[o],
            device_id=target, device_id_type=MESH,
        )
        c.start()
        self.open.append(c)
        return c

    def first(self):
        self.now = []
        for o in range(1, self.n_sib):
            to = lax.rem(self.sib + o, self.n_sib)
            rows = pl.ds(pl.multiple_of(to * self.chunk, 8), self.chunk)
            self.now.append(self.copy(self.src.at[rows], self.r1.at[o], 0, o, (self.leaf, to)))

    def second(self):
        rows = pl.ds(pl.multiple_of(self.sib * self.chunk, 8), self.chunk)
        total = self.src[rows, :]
        for o, c in enumerate(self.now, 1):
            c.wait_recv()
            total += self.r1[o]
        mine = self.r2.at[self.leaf]
        self.r2[self.leaf] = total
        self.now = []
        for o in range(1, self.n_leaf):
            to = lax.rem(self.leaf + o, self.n_leaf)
            self.now.append(self.copy(mine, mine, 1, o, (to, self.sib)))

    def third(self):
        for c in self.now:
            c.wait_recv()
        total = self.r2[0]
        for o in range(1, self.n_leaf):
            total += self.r2[o]
        mine = self.r3.at[self.sib]
        self.r3[self.sib] = total
        self.now = []
        for o in range(1, self.n_sib):
            to = lax.rem(self.sib + o, self.n_sib)
            self.now.append(self.copy(mine, mine, 2, o, (self.leaf, to)))

    def result(self):
        for c in self.now:
            c.wait_recv()
        return jnp.concatenate([self.r3[o] for o in range(self.n_sib)], axis=0)


def kernel(
    sizes, near, order, src, diag, low, nearby, sol, coef, *scratch
):
    n_leaf, n_sib = sizes
    leaf, sib = lax.axis_index("leaf"), lax.axis_index("sib")
    pos = leaf * n_sib + sib
    last = n_leaf * n_sib - 1
    leaf_dev, leaf_size = diag.shape[0], diag.shape[1]
    rank = low.shape[1]
    blocks = [slice(i * leaf_size, (i + 1) * leaf_size) for i in range(leaf_dev)]
    windows, scratch = scratch[: 2 * ITERS - 1], scratch[2 * ITERS - 1 :]
    h_send, h_recv, lifted, lifted_t, powers, x_first, work = scratch[:7]
    scratch = scratch[7:]
    sums = [Sum((leaf, sib), sizes, scratch[10 * i : 10 * i + 10]) for i in range(len(SUMS))]

    def place(p):
        return (p // n_sib, lax.rem(p, n_sib))

    right, left = place(jnp.minimum(pos + 1, last)), place(jnp.maximum(pos - 1, 0))
    has_right, has_left = pos < last, pos > 0

    barrier = pltpu.get_barrier_semaphore()
    for o in range(1, n_sib):
        pl.semaphore_signal(
            barrier, inc=1, device_id=(leaf, lax.rem(sib + o, n_sib)), device_id_type=MESH
        )
    for o in range(1, n_leaf):
        pl.semaphore_signal(
            barrier, inc=1, device_id=(lax.rem(leaf + o, n_leaf), sib), device_id_type=MESH
        )

    @pl.when(has_right)
    def _():
        pl.semaphore_signal(barrier, inc=1, device_id=right, device_id_type=MESH)

    @pl.when(has_left)
    def _():
        pl.semaphore_signal(barrier, inc=1, device_id=left, device_id_type=MESH)

    def halo(k):
        own = windows[k].at[leaf_dev : 2 * leaf_dev]
        up = pltpu.make_async_remote_copy(
            src_ref=own, dst_ref=windows[k].at[0:leaf_dev],
            send_sem=h_send.at[k, 0], recv_sem=h_recv.at[k, 0],
            device_id=right, device_id_type=MESH,
        )
        down = pltpu.make_async_remote_copy(
            src_ref=own, dst_ref=windows[k].at[2 * leaf_dev : 3 * leaf_dev],
            send_sem=h_send.at[k, 1], recv_sem=h_recv.at[k, 1],
            device_id=left, device_id_type=MESH,
        )
        return up, down

    def send_halo(k, values):
        for i in range(leaf_dev):
            windows[k][leaf_dev + i] = values[i].astype(jnp.bfloat16)
        up, down = halo(k)
        pl.when(has_right)(lambda: up.start())
        pl.when(has_left)(lambda: down.start())

    def wait_halo(k):
        up, down = halo(k)
        pl.when(has_left)(lambda: up.wait_recv())
        pl.when(has_right)(lambda: down.wait_recv())

    def near_apply(k):
        out = []
        for i in range(leaf_dev):
            total = None
            for m in range(near.shape[1]):
                t = jnp.clip(near[i, m] - (pos - 1) * leaf_dev, 0, 3 * leaf_dev - 1)
                part = jnp.dot(nearby[i, m], windows[k][t], preferred_element_type=jnp.float32)
                total = part if total is None else total + part
            out.append(total)
        return out

    def project(values):
        return sum(mm(lifted_t[:, blocks[i]], values[i]) for i in range(leaf_dev))

    core = jnp.zeros((rank, rank), jnp.float32)
    first = jnp.zeros((rank, src.shape[1]), jnp.float32)
    row_ids = lax.broadcasted_iota(jnp.int32, (leaf_size, leaf_size), 0)
    scaled = []
    for i, rows in enumerate(blocks):
        block = low[rows, :]
        up = mm(diag[i], block)
        lifted[rows, :] = up
        up_t = up.T
        lifted_t[:, rows] = up_t
        core += mm(up_t, block)
        local = order[i] - (pos * leaf_dev + i) * leaf_size
        pick = (row_ids == local).astype(jnp.float32)
        ordered = mm_t(pick, src[rows, :])
        scaled.append(mm(diag[i], ordered))
        first += mm(up_t, ordered)
    sums[0].src[0:rank, :] = core
    sums[0].src[rank:, :] = first

    sides = 1 - pos // last + (pos + last - 1) // last
    pl.semaphore_wait(barrier, n_sib + n_leaf - 2 + sides)

    sums[0].first()
    send_halo(0, [lifted[rows, :] for rows in blocks])
    sums[0].second()

    def power(j):
        wait_halo(j)
        image = near_apply(j)
        value = [-mm(diag[i], image[i]) for i in range(leaf_dev)]
        if j + 1 < ITERS - 1:
            send_halo(j + 1, value)
        for i, rows in enumerate(blocks):
            powers[j, rows, :] = value[i]
        sums[1].src[j * rank : (j + 1) * rank, :] = project(image)

    power(0)
    sums[0].third()
    power(1)
    both = sums[0].result()
    eye = lax.broadcasted_iota(jnp.int32, (rank, rank), 0) == lax.broadcasted_iota(
        jnp.int32, (rank, rank), 1
    )
    work[...] = both[:rank] + jnp.where(eye, 1.0, 0.0)
    invert(work)
    c_first = mm(work[...], both[rank:])
    coef[...] = c_first
    now = []
    for i, rows in enumerate(blocks):
        value = scaled[i] - mm(lifted[rows, :], c_first)
        x_first[rows, :] = value
        now.append(value)
    base = ITERS - 1
    send_halo(base, now)
    power(2)
    sums[1].first()
    for k in range(ITERS):
        wait_halo(base + k)
        image = near_apply(base + k)
        now = [x_first[rows, :] - mm(diag[i], image[i]) for i, rows in enumerate(blocks)]
        if k + 1 < ITERS:
            send_halo(base + k + 1, now)
        sums[2 + k].src[...] = project(image)
        sums[2 + k].first()
        if k == 0:
            sums[1].second()
        if k == 1:
            sums[1].third()
        if k >= 1:
            sums[1 + k].second()
        if k >= 2:
            sums[k].third()

    moments = sums[1].result()
    moment = [moments[j * rank : (j + 1) * rank] for j in range(ITERS - 1)]
    deltas = [None]

    def solve(k):
        total = -sums[1 + k].result()
        for j in range(k - 1):
            total += mm(moment[j], deltas[k - 1 - j])
        deltas.append(mm(work[...], total))

    solve(1)
    sums[5].second()
    sums[4].third()
    solve(2)
    solve(3)
    sums[5].third()

    def correct(i, j):
        basis = lifted[blocks[i], :] if j == 0 else powers[j - 1, blocks[i], :]
        return mm(basis, deltas[ITERS - j])

    now = [now[i] - sum(correct(i, j) for j in range(1, ITERS)) for i in range(leaf_dev)]
    solve(4)
    for i, rows in enumerate(blocks):
        sol[rows, :] = now[i] - correct(i, 0)
    coef[...] += deltas[ITERS]

    for s in sums:
        for c in s.open:
            c.wait_send()
    for k in range(2 * ITERS - 1):
        up, down = halo(k)
        pl.when(has_right)(lambda up=up: up.wait_send())
        pl.when(has_left)(lambda down=down: down.wait_send())


def on_device(sources, ordering, diagonal_inverse, low_rank, nearby_blocks, near_index):
    n_leaf, n_sib = lax.axis_size("leaf"), lax.axis_size("sib")
    leaf_dev, leaf_size = diagonal_inverse.shape[:2]
    rows, columns = sources.shape
    rank = low_rank.shape[1]
    f32 = jnp.float32
    scratch = [
        pltpu.VMEM((3 * leaf_dev, leaf_size, columns), jnp.bfloat16) for _ in range(2 * ITERS - 1)
    ]
    scratch += [
        pltpu.SemaphoreType.DMA((2 * ITERS - 1, 2)),
        pltpu.SemaphoreType.DMA((2 * ITERS - 1, 2)),
        pltpu.VMEM((rows, rank), f32),
        pltpu.VMEM((rank, rows), f32),
        pltpu.VMEM((ITERS - 1, rows, rank), f32),
        pltpu.VMEM((rows, columns), f32),
        pltpu.VMEM((rank, rank), f32),
    ]
    for count in SUMS:
        chunk = count * rank // n_sib
        scratch += [
            pltpu.VMEM((count * rank, columns), f32),
            pltpu.VMEM((n_sib, chunk, columns), f32),
            pltpu.VMEM((n_leaf, chunk, columns), f32),
            pltpu.VMEM((n_sib, chunk, columns), f32),
        ]
        for n in (n_sib, n_leaf, n_sib):
            scratch += [pltpu.SemaphoreType.DMA((n,)), pltpu.SemaphoreType.DMA((n,))]
    vmem = pl.BlockSpec(memory_space=pltpu.VMEM)
    return pl.pallas_call(
        functools.partial(kernel, (n_leaf, n_sib)),
        out_shape=(
            jax.ShapeDtypeStruct((rows, columns), f32),
            jax.ShapeDtypeStruct((rank, columns), f32),
        ),
        in_specs=[pl.BlockSpec(memory_space=pltpu.SMEM)] + [vmem] * 5,
        out_specs=(vmem, vmem),
        scratch_shapes=scratch,
        compiler_params=pltpu.CompilerParams(
            collective_id=0, has_side_effects=True, vmem_limit_bytes=48 * 1024 * 1024
        ),
    )(
        near_index,
        ordering.reshape(leaf_dev, 1, leaf_size),
        sources,
        diagonal_inverse,
        low_rank,
        nearby_blocks,
    )


def solution(mesh):
    placed = (
        P(("leaf", "sib"), None),
        P(("leaf", "sib")),
        P(("leaf", "sib"), None, None),
        P(("leaf", "sib"), None),
        P(("leaf", "sib"), None, None, None),
        P(("leaf", "sib"), None),
    )
    return jax.shard_map(
        on_device,
        mesh=mesh,
        in_specs=placed,
        out_specs=(P(("leaf", "sib"), None), P()),
        check_vma=False,
    )
```

```python
import functools

import jax
import jax.numpy as jnp
from jax import lax
from jax.experimental import pallas as pl
from jax.experimental.pallas import tpu as pltpu
from jax.sharding import PartitionSpec as P

ITERS = 4
MESH = pl.DeviceIdType.MESH
HIGH = lax.Precision.HIGHEST
COUNTS = (2, 2, 2) + (1,) * ITERS
PIVOTS = 8
LEVELS = 5


def mm(a, b):
    return jnp.dot(a, b, precision=HIGH, preferred_element_type=jnp.float32)


def mm_t(a, b):
    return lax.dot_general(
        a, b, (((0,), (0,)), ((), ())), precision=HIGH, preferred_element_type=jnp.float32
    )


def split(x):
    high = x.astype(jnp.bfloat16)
    return high, (x - high.astype(jnp.float32)).astype(jnp.bfloat16)


def guess(core, right):
    size = core.shape[0]
    eye = lax.broadcasted_iota(jnp.int32, (size, size), 0) == lax.broadcasted_iota(
        jnp.int32, (size, size), 1
    )
    bound = jnp.max(jnp.sum(jnp.abs(core), axis=1, keepdims=True), axis=0, keepdims=True)
    scale = 2.0 / (1.0 + bound)
    rest = jnp.where(eye, 1.0, 0.0) - core * scale
    value = right * scale
    for level in range(LEVELS):
        value += jnp.dot(rest, value, preferred_element_type=jnp.float32)
        if level + 1 < LEVELS:
            rest = jnp.dot(rest, rest, preferred_element_type=jnp.float32)
    return value


def eliminate(work, offsets):
    size = work.shape[0]
    lane = lax.broadcasted_iota(jnp.int32, (PIVOTS, size), 1)
    sub = lax.broadcasted_iota(jnp.int32, (PIVOTS, size), 0)
    wide = lax.broadcasted_iota(jnp.int32, (size, size), 1)
    for off in offsets:
        panel = work[off : off + PIVOTS, :]
        left = jnp.where(lane < off, -panel, panel)
        for j in range(PIVOTS):
            c = off + j
            inv = 1.0 / panel[j : j + 1, c : c + 1]
            row = jnp.where(lane == c, inv, panel[j : j + 1, :] * inv)
            rest = jnp.where(lane == c, 0.0, panel) - panel[:, c : c + 1] * row
            panel = jnp.where(sub == j, row, rest)
        inside = (wide >= off) & (wide < off + PIVOTS)
        work[...] = jnp.where(inside, 0.0, work[...]) - mm_t(left, panel)
        work[off : off + PIVOTS, :] = panel


def parted(n, sizes, last):
    n_leaf, n_sib = sizes
    return not last and (n // n_sib) % n_leaf == 0


class Sum:
    def __init__(self, me, sizes, refs):
        self.leaf, self.sib = me
        self.n_leaf, self.n_sib = sizes
        self.src, self.r1, self.t2, self.r2, self.r3, *self.sems = refs
        self.chunk = self.r1.shape[1]
        self.parts, self.piece = self.r3.shape[1:3]
        self.open, self.now = [], []
        self.steps = [self.scatter_sib]
        if self.parts > 1:
            self.steps += [self.scatter_leaf, self.gather_leaf, self.gather_sib]
        else:
            self.steps += [self.exchange_leaf, self.gather_sib]

    def step(self):
        if self.steps:
            work, self.steps = self.steps[0], self.steps[1:]
            work()

    def arrived(self):
        for c in self.now:
            c.wait_recv()
        self.now = []

    def copy(self, src, dst, phase, o, target):
        send, recv = self.sems[2 * phase], self.sems[2 * phase + 1]
        c = pltpu.make_async_remote_copy(
            src_ref=src, dst_ref=dst, send_sem=send.at[o], recv_sem=recv.at[o],
            device_id=target, device_id_type=MESH,
        )
        c.start()
        self.open.append(c)
        self.now.append(c)

    def sibs(self):
        for o in range(1, self.n_sib):
            to = lax.rem(self.sib + o, self.n_sib)
            yield o, to, (self.leaf, to)

    def leaves(self):
        for o in range(1, self.n_leaf):
            to = lax.rem(self.leaf + o, self.n_leaf)
            yield o, to, (to, self.sib)

    def scatter_sib(self):
        for o, to, place in self.sibs():
            rows = pl.ds(pl.multiple_of(to * self.chunk, 8), self.chunk)
            self.copy(self.src.at[rows], self.r1.at[o], 0, o, place)

    def own(self):
        rows = pl.ds(pl.multiple_of(self.sib * self.chunk, 8), self.chunk)
        total = self.src[rows, :]
        self.arrived()
        for o in range(1, self.n_sib):
            total += self.r1[o]
        return total

    def exchange_leaf(self):
        self.r2[self.leaf] = self.own()
        mine = self.r2.at[self.leaf]
        for o, to, place in self.leaves():
            self.copy(mine, mine, 1, o, place)

    def scatter_leaf(self):
        total = self.own()
        for o in range(self.n_leaf):
            self.t2[o] = total[o * self.piece : (o + 1) * self.piece]
        for o, to, place in self.leaves():
            self.copy(self.t2.at[to], self.r2.at[o], 1, o, place)

    def gather_leaf(self):
        self.arrived()
        total = self.t2[self.leaf]
        for o in range(1, self.n_leaf):
            total += self.r2[o]
        self.r3[self.sib, self.leaf] = total
        mine = self.r3.at[self.sib, self.leaf]
        for o, to, place in self.leaves():
            self.copy(mine, mine, 2, o, place)

    def gather_sib(self):
        self.arrived()
        if self.parts == 1:
            total = self.r2[0]
            for o in range(1, self.n_leaf):
                total += self.r2[o]
            self.r3[self.sib, 0] = total
        mine = self.r3.at[self.sib]
        for o, to, place in self.sibs():
            self.copy(mine, mine, 3, o, place)

    def result(self):
        while self.steps:
            self.step()
        self.arrived()
        return jnp.concatenate(
            [self.r3[s, l] for s in range(self.n_sib) for l in range(self.parts)], axis=0
        )


def kernel(
    sizes, near_in, order_in, src_in, diag_in, low_in, nearby_in, sol, coef, *scratch
):
    n_leaf, n_sib = sizes
    leaf, sib = lax.axis_index("leaf"), lax.axis_index("sib")
    pos = leaf * n_sib + sib
    last = n_leaf * n_sib - 1
    (near, order, src, diag, low, nearby), in_sem, scratch = scratch[:6], scratch[6], scratch[7:]
    loads = [
        pltpu.make_async_copy(a, b, in_sem.at[i])
        for i, (a, b) in enumerate(
            ((low_in, low), (diag_in, diag), (order_in, order), (src_in, src),
             (near_in, near), (nearby_in, nearby))
        )
    ]
    for c in loads:
        c.start()
    leaf_dev, leaf_size = diag.shape[0], diag.shape[1]
    rank = low.shape[1]
    columns = src.shape[1]
    blocks = [slice(i * leaf_size, (i + 1) * leaf_size) for i in range(leaf_dev)]
    windows, scratch = scratch[: 2 * ITERS], scratch[2 * ITERS :]
    h_send, h_recv, lifted, lifted_t, powers, x_first, work, d_high, d_low = scratch[:9]
    scratch = scratch[9:]
    sums = [Sum((leaf, sib), sizes, scratch[13 * i : 13 * i + 13]) for i in range(len(COUNTS))]
    moment_sums, image_sums = sums[1:3], sums[3:]

    def place(p):
        return (p // n_sib, lax.rem(p, n_sib))

    right, left = place(jnp.minimum(pos + 1, last)), place(jnp.maximum(pos - 1, 0))
    has_right, has_left = pos < last, pos > 0

    barrier = pltpu.get_barrier_semaphore()
    for o in range(1, n_sib):
        pl.semaphore_signal(
            barrier, inc=1, device_id=(leaf, lax.rem(sib + o, n_sib)), device_id_type=MESH
        )
    for o in range(1, n_leaf):
        pl.semaphore_signal(
            barrier, inc=1, device_id=(lax.rem(leaf + o, n_leaf), sib), device_id_type=MESH
        )

    @pl.when(has_right)
    def _():
        pl.semaphore_signal(barrier, inc=1, device_id=right, device_id_type=MESH)

    @pl.when(has_left)
    def _():
        pl.semaphore_signal(barrier, inc=1, device_id=left, device_id_type=MESH)

    def halo(k):
        own = windows[k].at[leaf_dev : 2 * leaf_dev]
        up = pltpu.make_async_remote_copy(
            src_ref=own, dst_ref=windows[k].at[0:leaf_dev],
            send_sem=h_send.at[k, 0], recv_sem=h_recv.at[k, 0],
            device_id=right, device_id_type=MESH,
        )
        down = pltpu.make_async_remote_copy(
            src_ref=own, dst_ref=windows[k].at[2 * leaf_dev : 3 * leaf_dev],
            send_sem=h_send.at[k, 1], recv_sem=h_recv.at[k, 1],
            device_id=left, device_id_type=MESH,
        )
        return up, down

    def send_halo(k, values):
        for i in range(leaf_dev):
            windows[k][leaf_dev + i] = values[i].astype(jnp.bfloat16)
        up, down = halo(k)
        pl.when(has_right)(lambda: up.start())
        pl.when(has_left)(lambda: down.start())

    def wait_halo(k):
        up, down = halo(k)
        pl.when(has_left)(lambda: up.wait_recv())
        pl.when(has_right)(lambda: down.wait_recv())

    def near_apply(k):
        out = []
        for i in range(leaf_dev):
            total = None
            for m in range(near.shape[1]):
                t = jnp.clip(near[i, m] - (pos - 1) * leaf_dev, 0, 3 * leaf_dev - 1)
                part = jnp.dot(nearby[i, m], windows[k][t], preferred_element_type=jnp.float32)
                total = part if total is None else total + part
            out.append(total)
        return out

    def project(values):
        return sum(mm(lifted_t[:, blocks[i]], values[i]) for i in range(leaf_dev))

    def inverse_times(i, v):
        high, rest = split(v)
        wide = jnp.dot(
            d_high[i], jnp.concatenate([high, rest], axis=1), preferred_element_type=jnp.float32
        )
        small = jnp.dot(d_low[i], high, preferred_element_type=jnp.float32)
        return wide[:, : v.shape[1]] + (wide[:, v.shape[1] :] + small)

    core = jnp.zeros((rank, rank), jnp.float32)
    first = jnp.zeros((rank, columns), jnp.float32)
    row_ids = lax.broadcasted_iota(jnp.int32, (leaf_size, leaf_size), 0)
    loads[0].wait()
    loads[1].wait()
    for i, rows in enumerate(blocks):
        d_high[i], d_low[i] = split(diag[i])
        block = low[rows, :]
        up = mm(diag[i], block)
        lifted[rows, :] = up
        up_t = up.T
        lifted_t[:, rows] = up_t
        core += mm(up_t, block)
    loads[2].wait()
    loads[3].wait()
    scaled = []
    for i, rows in enumerate(blocks):
        local = order[i] - (pos * leaf_dev + i) * leaf_size
        pick = (row_ids == local).astype(jnp.float32).T.astype(jnp.bfloat16)
        value = src[rows, :]
        high = value.astype(jnp.bfloat16)
        value = value - high.astype(jnp.float32)
        parts = jnp.concatenate([high, *split(value)], axis=1)
        parts = jnp.dot(pick, parts, preferred_element_type=jnp.float32)
        ordered = parts[:, :columns] + (
            parts[:, columns : 2 * columns] + parts[:, 2 * columns :]
        )
        scaled.append(inverse_times(i, ordered))
        first += mm(lifted_t[:, rows], ordered)
    sums[0].src[0:rank, :] = core
    sums[0].src[rank:, :] = first

    sides = 1 - pos // last + (pos + last - 1) // last
    pl.semaphore_wait(barrier, n_sib + n_leaf - 2 + sides)

    sums[0].step()
    send_halo(0, [lifted[rows, :] for rows in blocks])
    loads[4].wait()
    loads[5].wait()

    def power(j):
        wait_halo(j)
        image = near_apply(j)
        value = [-inverse_times(i, image[i]) for i in range(leaf_dev)]
        if j + 1 < ITERS:
            send_halo(j + 1, value)
        for i, rows in enumerate(blocks):
            powers[j, rows, :] = value[i]
        part = j % 2
        moment_sums[j // 2].src[part * rank : (part + 1) * rank, :] = project(image)
        if part:
            moment_sums[j // 2].step()

    sums[0].step()
    sums[0].step()
    power(0)
    both = sums[0].result()
    eye = lax.broadcasted_iota(jnp.int32, (rank, rank), 0) == lax.broadcasted_iota(
        jnp.int32, (rank, rank), 1
    )
    core = both[:rank] + jnp.where(eye, 1.0, 0.0)
    first = both[rank:]
    base = ITERS
    start = guess(core, first)
    now = []
    for i, rows in enumerate(blocks):
        value = scaled[i] - mm(lifted[rows, :], start)
        x_first[rows, :] = value
        now.append(value)
    send_halo(base, now)
    work[...] = core
    steps = list(range(0, rank, PIVOTS))
    share = len(steps) // ITERS

    power(1)
    eliminate(work, steps[:share])
    for k in range(ITERS):
        wait_halo(base + k)
        image = near_apply(base + k)
        now = [x_first[rows, :] - inverse_times(i, image[i]) for i, rows in enumerate(blocks)]
        if k + 1 < ITERS:
            send_halo(base + k + 1, now)
        image_sums[k].src[...] = project(image)
        image_sums[k].step()
        moment_sums[0].step()
        for j in range(k):
            image_sums[j].step()
        if k >= 2:
            moment_sums[1].step()
        if k + 2 < ITERS:
            power(k + 2)
        if k + 1 < ITERS:
            end = (k + 2) * share if k + 2 < ITERS else len(steps)
            eliminate(work, steps[(k + 1) * share : end])

    inverse = work[...]
    deltas = [mm(inverse, first) - start]
    moments = moment_sums[0].result()
    moment = [moments[:rank], moments[rank:]]

    def known(k):
        return sum(mm(moment[j], deltas[k - 1 - j]) for j in range(k))

    def solve(k):
        deltas.append(deltas[0] + mm(inverse, known(k) - image_sums[k - 1].result()))

    solve(1)
    image_sums[-1].step()
    for s in (moment_sums[1], *image_sums[1:-1]):
        s.step()
    solve(2)
    image_sums[-1].step()
    moments = moment_sums[1].result()
    moment += [moments[:rank], moments[rank:]]
    solve(3)

    def correct(i, j):
        basis = lifted[blocks[i], :] if j == 0 else powers[j - 1, blocks[i], :]
        return mm(basis, deltas[ITERS - j])

    now = [now[i] - sum(correct(i, j) for j in range(1, ITERS + 1)) for i in range(leaf_dev)]
    solve(4)
    for i, rows in enumerate(blocks):
        sol[rows, :] = now[i] - correct(i, 0)
    coef[...] = start + deltas[ITERS]

    for s in sums:
        for c in s.open:
            c.wait_send()
    for k in range(2 * ITERS):
        up, down = halo(k)
        pl.when(has_right)(lambda up=up: up.wait_send())
        pl.when(has_left)(lambda down=down: down.wait_send())


def on_device(sources, ordering, diagonal_inverse, low_rank, nearby_blocks, near_index):
    n_leaf, n_sib = lax.axis_size("leaf"), lax.axis_size("sib")
    leaf_dev, leaf_size = diagonal_inverse.shape[:2]
    rows, columns = sources.shape
    rank = low_rank.shape[1]
    f32 = jnp.float32
    operands = (
        near_index,
        ordering.reshape(leaf_dev, 1, leaf_size),
        sources,
        diagonal_inverse,
        low_rank,
        nearby_blocks,
    )
    scratch = [pltpu.SMEM(near_index.shape, near_index.dtype)]
    scratch += [pltpu.VMEM(x.shape, x.dtype) for x in operands[1:]]
    scratch += [pltpu.SemaphoreType.DMA((len(operands),))]
    scratch += [
        pltpu.VMEM((3 * leaf_dev, leaf_size, columns), jnp.bfloat16) for _ in range(2 * ITERS)
    ]
    scratch += [
        pltpu.SemaphoreType.DMA((2 * ITERS, 2)),
        pltpu.SemaphoreType.DMA((2 * ITERS, 2)),
        pltpu.VMEM((rows, rank), f32),
        pltpu.VMEM((rank, rows), f32),
        pltpu.VMEM((ITERS, rows, rank), f32),
        pltpu.VMEM((rows, columns), f32),
        pltpu.VMEM((rank, rank), f32),
        pltpu.VMEM(diagonal_inverse.shape, jnp.bfloat16),
        pltpu.VMEM(diagonal_inverse.shape, jnp.bfloat16),
    ]
    for n, count in enumerate(COUNTS):
        total = count * rank
        chunk = total // n_sib
        cut = parted(total, (n_leaf, n_sib), n + 1 == len(COUNTS))
        parts = n_leaf if cut else 1
        piece = chunk // parts
        scratch += [
            pltpu.VMEM((total, columns), f32),
            pltpu.VMEM((n_sib, chunk, columns), f32),
            pltpu.VMEM((parts, piece, columns), f32),
            pltpu.VMEM((n_leaf, piece, columns), f32),
            pltpu.VMEM((n_sib, parts, piece, columns), f32),
        ]
        for n in (n_sib, n_leaf, n_leaf, n_sib):
            scratch += [pltpu.SemaphoreType.DMA((n,)), pltpu.SemaphoreType.DMA((n,))]
    vmem = pl.BlockSpec(memory_space=pltpu.VMEM)
    return pl.pallas_call(
        functools.partial(kernel, (n_leaf, n_sib)),
        out_shape=(
            jax.ShapeDtypeStruct((rows, columns), f32),
            jax.ShapeDtypeStruct((rank, columns), f32),
        ),
        in_specs=[pl.BlockSpec(memory_space=pl.ANY)] * len(operands),
        out_specs=(vmem, vmem),
        scratch_shapes=scratch,
        compiler_params=pltpu.CompilerParams(
            collective_id=0, has_side_effects=True, vmem_limit_bytes=62 * 1024 * 1024
        ),
    )(*operands)


def solution(mesh):
    placed = (
        P(("leaf", "sib"), None),
        P(("leaf", "sib")),
        P(("leaf", "sib"), None, None),
        P(("leaf", "sib"), None),
        P(("leaf", "sib"), None, None, None),
        P(("leaf", "sib"), None),
    )
    return jax.shard_map(
        on_device,
        mesh=mesh,
        in_specs=placed,
        out_specs=(P(("leaf", "sib"), None), P()),
        check_vma=False,
    )
```

```python
import functools

import jax
import jax.numpy as jnp
from jax import lax
from jax.experimental import pallas as pl
from jax.experimental.pallas import tpu as pltpu
from jax.sharding import PartitionSpec as P

ITERS = 4
MESH = pl.DeviceIdType.MESH
HIGH = lax.Precision.HIGHEST
COUNTS = (2, 2, 2) + (1,) * ITERS
PIVOTS = 16
LEVELS = 5


def mm(a, b):
    return jnp.dot(a, b, precision=HIGH, preferred_element_type=jnp.float32)


def mm_t(a, b):
    return lax.dot_general(
        a, b, (((0,), (0,)), ((), ())), precision=HIGH, preferred_element_type=jnp.float32
    )


def split(x):
    high = x.astype(jnp.bfloat16)
    return high, (x - high.astype(jnp.float32)).astype(jnp.bfloat16)


def guess(core, right):
    size = core.shape[0]
    eye = lax.broadcasted_iota(jnp.int32, (size, size), 0) == lax.broadcasted_iota(
        jnp.int32, (size, size), 1
    )
    bound = jnp.max(jnp.sum(jnp.abs(core), axis=1, keepdims=True), axis=0, keepdims=True)
    scale = 2.0 / (1.0 + bound)
    rest = jnp.where(eye, 1.0, 0.0) - core * scale
    value = right * scale
    for level in range(LEVELS):
        value += jnp.dot(rest, value, preferred_element_type=jnp.float32)
        if level + 1 < LEVELS:
            rest = jnp.dot(rest, rest, preferred_element_type=jnp.float32)
    return value


def split3(x):
    high = x.astype(jnp.bfloat16)
    return (high, *split(x - high.astype(jnp.float32)))


def eliminate(work, offsets):
    size = work.shape[0]
    lane = lax.broadcasted_iota(jnp.int32, (PIVOTS, size), 1)
    sub = lax.broadcasted_iota(jnp.int32, (PIVOTS, size), 0)
    wide = lax.broadcasted_iota(jnp.int32, (size, size), 1)
    for off in offsets:
        panel = work[off : off + PIVOTS, :]
        left = jnp.where(lane < off, -panel, panel)
        cols = [
            jnp.broadcast_to(panel[:, off + j : off + j + 1], panel.shape) for j in range(PIVOTS)
        ]
        inside = (lane >= off) & (lane < off + PIVOTS)
        panel = jnp.where(inside, jnp.where(lane == off + sub, 1.0, 0.0), panel)
        for j in range(PIVOTS):
            inv = 1.0 / cols[j][j : j + 1, :]
            row = panel[j : j + 1, :] * inv
            panel = jnp.where(sub == j, row, panel - cols[j] * row)
            for m in range(j + 1, PIVOTS):
                row = cols[m][j : j + 1, :] * inv
                cols[m] = jnp.where(sub == j, row, cols[m] - cols[j] * row)
        h, m, l = split3(left.T)
        rh, rm, rl = split3(panel)
        update = jnp.dot(
            jnp.concatenate([h, h, m, h, l, m], axis=1),
            jnp.concatenate([rh, rm, rh, rl, rh, rm], axis=0),
            preferred_element_type=jnp.float32,
        )
        inside = (wide >= off) & (wide < off + PIVOTS)
        work[...] = jnp.where(inside, 0.0, work[...]) - update
        work[off : off + PIVOTS, :] = panel


def parted(n, sizes, last):
    n_leaf, n_sib = sizes
    return not last and (n // n_sib) % n_leaf == 0


class Sum:
    def __init__(self, me, sizes, refs):
        self.leaf, self.sib = me
        self.n_leaf, self.n_sib = sizes
        self.src, self.r1, self.t2, self.r2, self.r3, *self.sems = refs
        self.chunk = self.r1.shape[1]
        self.parts, self.piece = self.r3.shape[1:3]
        self.open, self.now = [], []
        self.steps = [self.scatter_sib]
        if self.parts > 1:
            self.steps += [self.scatter_leaf, self.gather_leaf, self.gather_sib]
        else:
            self.steps += [self.exchange_leaf, self.gather_sib]

    def step(self):
        if self.steps:
            work, self.steps = self.steps[0], self.steps[1:]
            work()

    def arrived(self):
        for c in self.now:
            c.wait_recv()
        self.now = []

    def copy(self, src, dst, phase, o, target):
        send, recv = self.sems[2 * phase], self.sems[2 * phase + 1]
        c = pltpu.make_async_remote_copy(
            src_ref=src, dst_ref=dst, send_sem=send.at[o], recv_sem=recv.at[o],
            device_id=target, device_id_type=MESH,
        )
        c.start()
        self.open.append(c)
        self.now.append(c)

    def sibs(self):
        for o in range(1, self.n_sib):
            to = lax.rem(self.sib + o, self.n_sib)
            yield o, to, (self.leaf, to)

    def leaves(self):
        for o in range(1, self.n_leaf):
            to = lax.rem(self.leaf + o, self.n_leaf)
            yield o, to, (to, self.sib)

    def scatter_sib(self):
        for o, to, place in self.sibs():
            rows = pl.ds(pl.multiple_of(to * self.chunk, 8), self.chunk)
            self.copy(self.src.at[rows], self.r1.at[o], 0, o, place)

    def own(self):
        rows = pl.ds(pl.multiple_of(self.sib * self.chunk, 8), self.chunk)
        total = self.src[rows, :]
        self.arrived()
        for o in range(1, self.n_sib):
            total += self.r1[o]
        return total

    def exchange_leaf(self):
        self.r2[self.leaf] = self.own()
        mine = self.r2.at[self.leaf]
        for o, to, place in self.leaves():
            self.copy(mine, mine, 1, o, place)

    def scatter_leaf(self):
        total = self.own()
        for o in range(self.n_leaf):
            self.t2[o] = total[o * self.piece : (o + 1) * self.piece]
        for o, to, place in self.leaves():
            self.copy(self.t2.at[to], self.r2.at[o], 1, o, place)

    def gather_leaf(self):
        self.arrived()
        total = self.t2[self.leaf]
        for o in range(1, self.n_leaf):
            total += self.r2[o]
        self.r3[self.sib, self.leaf] = total
        mine = self.r3.at[self.sib, self.leaf]
        for o, to, place in self.leaves():
            self.copy(mine, mine, 2, o, place)

    def gather_sib(self):
        self.arrived()
        if self.parts == 1:
            total = self.r2[0]
            for o in range(1, self.n_leaf):
                total += self.r2[o]
            self.r3[self.sib, 0] = total
        mine = self.r3.at[self.sib]
        for o, to, place in self.sibs():
            self.copy(mine, mine, 3, o, place)

    def result(self):
        while self.steps:
            self.step()
        self.arrived()
        return jnp.concatenate(
            [self.r3[s, l] for s in range(self.n_sib) for l in range(self.parts)], axis=0
        )


def kernel(
    sizes, near_in, order_in, src_in, diag_in, low_in, nearby_in, sol, coef, *scratch
):
    n_leaf, n_sib = sizes
    leaf, sib = lax.axis_index("leaf"), lax.axis_index("sib")
    pos = leaf * n_sib + sib
    last = n_leaf * n_sib - 1
    (near, order, src, diag, low, nearby), in_sem, scratch = scratch[:6], scratch[6], scratch[7:]
    loads = [
        pltpu.make_async_copy(a, b, in_sem.at[i])
        for i, (a, b) in enumerate(
            ((low_in, low), (diag_in, diag), (order_in, order), (src_in, src),
             (near_in, near), (nearby_in, nearby))
        )
    ]
    for c in loads:
        c.start()
    leaf_dev, leaf_size = diag.shape[0], diag.shape[1]
    rank = low.shape[1]
    columns = src.shape[1]
    blocks = [slice(i * leaf_size, (i + 1) * leaf_size) for i in range(leaf_dev)]
    windows, scratch = scratch[: 2 * ITERS], scratch[2 * ITERS :]
    h_send, h_recv, lifted, lifted_t, powers, x_first, work, d_high, d_low = scratch[:9]
    scratch = scratch[9:]
    sums = [Sum((leaf, sib), sizes, scratch[13 * i : 13 * i + 13]) for i in range(len(COUNTS))]
    moment_sums, image_sums = sums[1:3], sums[3:]

    def place(p):
        return (p // n_sib, lax.rem(p, n_sib))

    right, left = place(jnp.minimum(pos + 1, last)), place(jnp.maximum(pos - 1, 0))
    has_right, has_left = pos < last, pos > 0

    barrier = pltpu.get_barrier_semaphore()
    for o in range(1, n_sib):
        pl.semaphore_signal(
            barrier, inc=1, device_id=(leaf, lax.rem(sib + o, n_sib)), device_id_type=MESH
        )
    for o in range(1, n_leaf):
        pl.semaphore_signal(
            barrier, inc=1, device_id=(lax.rem(leaf + o, n_leaf), sib), device_id_type=MESH
        )

    @pl.when(has_right)
    def _():
        pl.semaphore_signal(barrier, inc=1, device_id=right, device_id_type=MESH)

    @pl.when(has_left)
    def _():
        pl.semaphore_signal(barrier, inc=1, device_id=left, device_id_type=MESH)

    def halo(k, i):
        own = windows[k].at[leaf_dev + i]
        up = pltpu.make_async_remote_copy(
            src_ref=own, dst_ref=windows[k].at[i],
            send_sem=h_send.at[k, 0, i], recv_sem=h_recv.at[k, 0, i],
            device_id=right, device_id_type=MESH,
        )
        down = pltpu.make_async_remote_copy(
            src_ref=own, dst_ref=windows[k].at[2 * leaf_dev + i],
            send_sem=h_send.at[k, 1, i], recv_sem=h_recv.at[k, 1, i],
            device_id=left, device_id_type=MESH,
        )
        return up, down

    def send_block(k, i, value):
        windows[k][leaf_dev + i] = value.astype(jnp.bfloat16)
        up, down = halo(k, i)
        pl.when(has_right)(lambda: up.start())
        pl.when(has_left)(lambda: down.start())

    def wait_halo(k):
        @pl.when(has_left)
        def _():
            for i in range(leaf_dev):
                halo(k, i)[0].wait_recv()

        @pl.when(has_right)
        def _():
            for i in range(leaf_dev):
                halo(k, i)[1].wait_recv()

    def near_apply(k, i):
        total = None
        for m in range(near.shape[1]):
            t = jnp.clip(near[i, m] - (pos - 1) * leaf_dev, 0, 3 * leaf_dev - 1)
            part = jnp.dot(nearby[i, m], windows[k][t], preferred_element_type=jnp.float32)
            total = part if total is None else total + part
        return total

    def project(values):
        return sum(mm(lifted_t[:, blocks[i]], values[i]) for i in range(leaf_dev))

    def inverse_times(i, v):
        high, rest = split(v)
        wide = jnp.dot(
            d_high[i], jnp.concatenate([high, rest], axis=1), preferred_element_type=jnp.float32
        )
        small = jnp.dot(d_low[i], high, preferred_element_type=jnp.float32)
        return wide[:, : v.shape[1]] + (wide[:, v.shape[1] :] + small)

    core = jnp.zeros((rank, rank), jnp.float32)
    first = jnp.zeros((rank, columns), jnp.float32)
    row_ids = lax.broadcasted_iota(jnp.int32, (leaf_size, leaf_size), 0)
    loads[0].wait()
    loads[1].wait()
    for i, rows in enumerate(blocks):
        d_high[i], d_low[i] = split(diag[i])
        block = low[rows, :]
        up = mm(diag[i], block)
        lifted[rows, :] = up
        up_t = up.T
        lifted_t[:, rows] = up_t
        core += mm(up_t, block)
    sides = 1 - pos // last + (pos + last - 1) // last
    pl.semaphore_wait(barrier, n_sib + n_leaf - 2 + sides)
    for i, rows in enumerate(blocks):
        send_block(0, i, lifted[rows, :])
    loads[2].wait()
    loads[3].wait()
    scaled = []
    for i, rows in enumerate(blocks):
        local = order[i] - (pos * leaf_dev + i) * leaf_size
        pick = (row_ids == local).astype(jnp.float32).T.astype(jnp.bfloat16)
        value = src[rows, :]
        high = value.astype(jnp.bfloat16)
        value = value - high.astype(jnp.float32)
        parts = jnp.concatenate([high, *split(value)], axis=1)
        parts = jnp.dot(pick, parts, preferred_element_type=jnp.float32)
        ordered = parts[:, :columns] + (
            parts[:, columns : 2 * columns] + parts[:, 2 * columns :]
        )
        scaled.append(inverse_times(i, ordered))
        first += mm(lifted_t[:, rows], ordered)
    sums[0].src[0:rank, :] = core
    sums[0].src[rank:, :] = first

    sums[0].step()
    loads[4].wait()
    loads[5].wait()

    def power(j):
        wait_halo(j)
        image = []
        for i, rows in enumerate(blocks):
            image.append(near_apply(j, i))
            value = -inverse_times(i, image[i])
            powers[j, rows, :] = value
            if j + 1 < ITERS:
                send_block(j + 1, i, value)
        part = j % 2
        moment_sums[j // 2].src[part * rank : (part + 1) * rank, :] = project(image)
        if part:
            moment_sums[j // 2].step()

    sums[0].step()
    sums[0].step()
    power(0)
    both = sums[0].result()
    eye = lax.broadcasted_iota(jnp.int32, (rank, rank), 0) == lax.broadcasted_iota(
        jnp.int32, (rank, rank), 1
    )
    core = both[:rank] + jnp.where(eye, 1.0, 0.0)
    first = both[rank:]
    base = ITERS
    start = guess(core, first)
    now = []
    for i, rows in enumerate(blocks):
        value = scaled[i] - mm(lifted[rows, :], start)
        send_block(base, i, value)
        x_first[rows, :] = value
        now.append(value)
    work[...] = core
    steps = list(range(0, rank, PIVOTS))
    share = len(steps) // ITERS

    power(1)
    eliminate(work, steps[:share])
    for k in range(ITERS):
        wait_halo(base + k)
        image, now = [], []
        for i, rows in enumerate(blocks):
            image.append(near_apply(base + k, i))
            now.append(x_first[rows, :] - inverse_times(i, image[i]))
            if k + 1 < ITERS:
                send_block(base + k + 1, i, now[i])
        image_sums[k].src[...] = project(image)
        image_sums[k].step()
        moment_sums[0].step()
        for j in range(k):
            image_sums[j].step()
        if k >= 2:
            moment_sums[1].step()
        if k + 2 < ITERS:
            power(k + 2)
        if k + 1 < ITERS:
            end = (k + 2) * share if k + 2 < ITERS else len(steps)
            eliminate(work, steps[(k + 1) * share : end])

    inverse = work[...]
    deltas = [mm(inverse, first) - start]
    moments = moment_sums[0].result()
    moment = [moments[:rank], moments[rank:]]

    def known(k):
        return sum(mm(moment[j], deltas[k - 1 - j]) for j in range(k))

    def solve(k):
        deltas.append(deltas[0] + mm(inverse, known(k) - image_sums[k - 1].result()))

    solve(1)
    image_sums[-1].step()
    for s in (moment_sums[1], *image_sums[1:-1]):
        s.step()
    solve(2)
    image_sums[-1].step()
    moments = moment_sums[1].result()
    moment += [moments[:rank], moments[rank:]]
    solve(3)

    part = deltas[0] + mm(inverse, known(ITERS))
    deltas.append(part)
    for i, rows in enumerate(blocks):
        value = now[i] - mm(lifted[rows, :], part)
        for j in range(1, ITERS + 1):
            value -= mm(powers[j - 1, rows, :], deltas[ITERS - j])
        sol[rows, :] = value
        lifted[rows, :] = mm(lifted[rows, :], inverse)
    final = image_sums[-1].result()
    for rows in blocks:
        sol[rows, :] += mm(lifted[rows, :], final)
    coef[...] = start + part - mm(inverse, final)

    for s in sums:
        for c in s.open:
            c.wait_send()
    for k in range(2 * ITERS):
        for i in range(leaf_dev):
            up, down = halo(k, i)
            pl.when(has_right)(lambda up=up: up.wait_send())
            pl.when(has_left)(lambda down=down: down.wait_send())


def on_device(sources, ordering, diagonal_inverse, low_rank, nearby_blocks, near_index):
    n_leaf, n_sib = lax.axis_size("leaf"), lax.axis_size("sib")
    leaf_dev, leaf_size = diagonal_inverse.shape[:2]
    rows, columns = sources.shape
    rank = low_rank.shape[1]
    f32 = jnp.float32
    operands = (
        near_index,
        ordering.reshape(leaf_dev, 1, leaf_size),
        sources,
        diagonal_inverse,
        low_rank,
        nearby_blocks,
    )
    scratch = [pltpu.SMEM(near_index.shape, near_index.dtype)]
    scratch += [pltpu.VMEM(x.shape, x.dtype) for x in operands[1:]]
    scratch += [pltpu.SemaphoreType.DMA((len(operands),))]
    scratch += [
        pltpu.VMEM((3 * leaf_dev, leaf_size, columns), jnp.bfloat16) for _ in range(2 * ITERS)
    ]
    scratch += [
        pltpu.SemaphoreType.DMA((2 * ITERS, 2, leaf_dev)),
        pltpu.SemaphoreType.DMA((2 * ITERS, 2, leaf_dev)),
        pltpu.VMEM((rows, rank), f32),
        pltpu.VMEM((rank, rows), f32),
        pltpu.VMEM((ITERS, rows, rank), f32),
        pltpu.VMEM((rows, columns), f32),
        pltpu.VMEM((rank, rank), f32),
        pltpu.VMEM(diagonal_inverse.shape, jnp.bfloat16),
        pltpu.VMEM(diagonal_inverse.shape, jnp.bfloat16),
    ]
    for n, count in enumerate(COUNTS):
        total = count * rank
        chunk = total // n_sib
        cut = parted(total, (n_leaf, n_sib), n + 1 == len(COUNTS))
        parts = n_leaf if cut else 1
        piece = chunk // parts
        scratch += [
            pltpu.VMEM((total, columns), f32),
            pltpu.VMEM((n_sib, chunk, columns), f32),
            pltpu.VMEM((parts, piece, columns), f32),
            pltpu.VMEM((n_leaf, piece, columns), f32),
            pltpu.VMEM((n_sib, parts, piece, columns), f32),
        ]
        for n in (n_sib, n_leaf, n_leaf, n_sib):
            scratch += [pltpu.SemaphoreType.DMA((n,)), pltpu.SemaphoreType.DMA((n,))]
    vmem = pl.BlockSpec(memory_space=pltpu.VMEM)
    return pl.pallas_call(
        functools.partial(kernel, (n_leaf, n_sib)),
        out_shape=(
            jax.ShapeDtypeStruct((rows, columns), f32),
            jax.ShapeDtypeStruct((rank, columns), f32),
        ),
        in_specs=[pl.BlockSpec(memory_space=pl.ANY)] * len(operands),
        out_specs=(vmem, vmem),
        scratch_shapes=scratch,
        compiler_params=pltpu.CompilerParams(
            collective_id=0, has_side_effects=True, vmem_limit_bytes=62 * 1024 * 1024
        ),
    )(*operands)


def solution(mesh):
    placed = (
        P(("leaf", "sib"), None),
        P(("leaf", "sib")),
        P(("leaf", "sib"), None, None),
        P(("leaf", "sib"), None),
        P(("leaf", "sib"), None, None, None),
        P(("leaf", "sib"), None),
    )
    return jax.shard_map(
        on_device,
        mesh=mesh,
        in_specs=placed,
        out_specs=(P(("leaf", "sib"), None), P()),
        check_vma=False,
    )
```

```python
import functools

import jax
import jax.numpy as jnp
from jax import lax
from jax.experimental import pallas as pl
from jax.experimental.pallas import tpu as pltpu
from jax.sharding import PartitionSpec as P

ITERS = 4
MESH = pl.DeviceIdType.MESH
HIGH = lax.Precision.HIGHEST
COUNTS = (2, ITERS, 2, 2)
PIVOTS = 16
LEVELS = 5


def mm(a, b):
    return jnp.dot(a, b, precision=HIGH, preferred_element_type=jnp.float32)


def mm_t(a, b):
    return lax.dot_general(
        a, b, (((0,), (0,)), ((), ())), precision=HIGH, preferred_element_type=jnp.float32
    )


def split(x):
    high = x.astype(jnp.bfloat16)
    return high, (x - high.astype(jnp.float32)).astype(jnp.bfloat16)


def guess(core, right):
    size = core.shape[0]
    eye = lax.broadcasted_iota(jnp.int32, (size, size), 0) == lax.broadcasted_iota(
        jnp.int32, (size, size), 1
    )
    bound = jnp.max(jnp.sum(jnp.abs(core), axis=1, keepdims=True), axis=0, keepdims=True)
    scale = 2.0 / (1.0 + bound)
    rest = jnp.where(eye, 1.0, 0.0) - core * scale
    value = right * scale
    for level in range(LEVELS):
        value += jnp.dot(rest, value, preferred_element_type=jnp.float32)
        if level + 1 < LEVELS:
            rest = jnp.dot(rest, rest, preferred_element_type=jnp.float32)
    return value


def split3(x):
    high = x.astype(jnp.bfloat16)
    return (high, *split(x - high.astype(jnp.float32)))


def eliminate(work, offsets):
    size = work.shape[0]
    lane = lax.broadcasted_iota(jnp.int32, (PIVOTS, size), 1)
    sub = lax.broadcasted_iota(jnp.int32, (PIVOTS, size), 0)
    wide = lax.broadcasted_iota(jnp.int32, (size, size), 1)
    for off in offsets:
        panel = work[off : off + PIVOTS, :]
        left = jnp.where(lane < off, -panel, panel)
        cols = [
            jnp.broadcast_to(panel[:, off + j : off + j + 1], panel.shape) for j in range(PIVOTS)
        ]
        inside = (lane >= off) & (lane < off + PIVOTS)
        panel = jnp.where(inside, jnp.where(lane == off + sub, 1.0, 0.0), panel)
        for j in range(PIVOTS):
            inv = 1.0 / cols[j][j : j + 1, :]
            row = panel[j : j + 1, :] * inv
            panel = jnp.where(sub == j, row, panel - cols[j] * row)
            for m in range(j + 1, PIVOTS):
                row = cols[m][j : j + 1, :] * inv
                cols[m] = jnp.where(sub == j, row, cols[m] - cols[j] * row)
        h, m, l = split3(left.T)
        rh, rm, rl = split3(panel)
        update = jnp.dot(
            jnp.concatenate([h, h, m, h, l, m], axis=1),
            jnp.concatenate([rh, rm, rh, rl, rh, rm], axis=0),
            preferred_element_type=jnp.float32,
        )
        inside = (wide >= off) & (wide < off + PIVOTS)
        work[...] = jnp.where(inside, 0.0, work[...]) - update
        work[off : off + PIVOTS, :] = panel


def parted(n, sizes):
    n_leaf, n_sib = sizes
    return (n // n_sib) % n_leaf == 0


class Sum:
    def __init__(self, me, sizes, refs):
        self.leaf, self.sib = me
        self.n_leaf, self.n_sib = sizes
        self.src, self.r1, self.t2, self.r2, self.r3, self.send, self.recv = refs
        self.chunk = self.r1.shape[1]
        self.parts, self.piece = self.r3.shape[1:3]
        self.open, self.now = [], None
        self.steps = [self.scatter_sib]
        if self.parts > 1:
            self.steps += [self.scatter_leaf, self.gather_leaf, self.gather_sib]
        else:
            self.steps += [self.exchange_leaf, self.gather_sib]

    def step(self):
        if self.steps:
            work, self.steps = self.steps[0], self.steps[1:]
            work()

    def arrived(self):
        phase, bulk = self.now
        pltpu.make_async_copy(bulk, bulk, self.recv.at[phase]).wait()

    def sent(self):
        for phase, bulk in self.open:
            pltpu.make_async_copy(bulk, bulk, self.send.at[phase]).wait()
        self.open = []

    def bulk(self, phase, ref):
        self.now = (phase, ref)
        self.open.append(self.now)

    def copy(self, src, dst, phase, target):
        pltpu.make_async_remote_copy(
            src_ref=src, dst_ref=dst, send_sem=self.send.at[phase], recv_sem=self.recv.at[phase],
            device_id=target, device_id_type=MESH,
        ).start()

    def sibs(self):
        for o in range(1, self.n_sib):
            to = lax.rem(self.sib + o, self.n_sib)
            yield o, to, (self.leaf, to)

    def leaves(self):
        for o in range(1, self.n_leaf):
            to = lax.rem(self.leaf + o, self.n_leaf)
            yield o, to, (to, self.sib)

    def scatter_sib(self):
        for o, to, place in self.sibs():
            rows = pl.ds(pl.multiple_of(to * self.chunk, 8), self.chunk)
            self.copy(self.src.at[rows], self.r1.at[o], 0, place)
        self.bulk(0, self.r1.at[1:])

    def own(self):
        rows = pl.ds(pl.multiple_of(self.sib * self.chunk, 8), self.chunk)
        total = self.src[rows, :]
        self.arrived()
        for o in range(1, self.n_sib):
            total += self.r1[o]
        return total

    def exchange_leaf(self):
        self.r2[self.leaf] = self.own()
        mine = self.r2.at[self.leaf]
        for o, to, place in self.leaves():
            self.copy(mine, mine, 1, place)
        self.bulk(1, self.r2.at[1:])

    def scatter_leaf(self):
        total = self.own()
        for o in range(self.n_leaf):
            self.t2[o] = total[o * self.piece : (o + 1) * self.piece]
        for o, to, place in self.leaves():
            self.copy(self.t2.at[to], self.r2.at[o], 1, place)
        self.bulk(1, self.r2.at[1:])

    def gather_leaf(self):
        self.arrived()
        total = self.t2[self.leaf]
        for o in range(1, self.n_leaf):
            total += self.r2[o]
        self.r3[self.sib, self.leaf] = total
        mine = self.r3.at[self.sib, self.leaf]
        for o, to, place in self.leaves():
            self.copy(mine, mine, 2, place)
        self.bulk(2, self.r3.at[0, 1:])

    def gather_sib(self):
        self.arrived()
        if self.parts == 1:
            total = self.r2[0]
            for o in range(1, self.n_leaf):
                total += self.r2[o]
            self.r3[self.sib, 0] = total
        mine = self.r3.at[self.sib]
        for o, to, place in self.sibs():
            self.copy(mine, mine, 3, place)
        self.bulk(3, self.r3.at[1:])

    def result(self):
        while self.steps:
            self.step()
        self.arrived()
        return jnp.concatenate(
            [self.r3[s, l] for s in range(self.n_sib) for l in range(self.parts)], axis=0
        )


def kernel(
    sizes, near_in, order_in, src_in, diag_in, low_in, nearby_in, sol, coef, *scratch
):
    n_leaf, n_sib = sizes
    leaf, sib = lax.axis_index("leaf"), lax.axis_index("sib")
    pos = leaf * n_sib + sib
    last = n_leaf * n_sib - 1
    (near, order, src, diag, low, nearby), in_sem, scratch = scratch[:6], scratch[6], scratch[7:]
    loads = [
        pltpu.make_async_copy(a, b, in_sem.at[i])
        for i, (a, b) in enumerate(
            ((low_in, low), (diag_in, diag), (order_in, order), (src_in, src),
             (near_in, near), (nearby_in, nearby))
        )
    ]
    for c in loads:
        c.start()
    leaf_dev, leaf_size = diag.shape[0], diag.shape[1]
    rank = low.shape[1]
    columns = src.shape[1]
    blocks = [slice(i * leaf_size, (i + 1) * leaf_size) for i in range(leaf_dev)]
    windows, scratch = scratch[: 2 * ITERS], scratch[2 * ITERS :]
    h_send, h_recv, lifted, lifted_t, powers, x_first, work, d_high, d_low = scratch[:9]
    scratch = scratch[9:]
    sums = [Sum((leaf, sib), sizes, scratch[7 * i : 7 * i + 7]) for i in range(len(COUNTS))]
    moment_sum, early, late = sums[1:]

    def place(p):
        return (p // n_sib, lax.rem(p, n_sib))

    right, left = place(jnp.minimum(pos + 1, last)), place(jnp.maximum(pos - 1, 0))
    has_right, has_left = pos < last, pos > 0

    barrier = pltpu.get_barrier_semaphore()
    for o in range(1, n_sib):
        pl.semaphore_signal(
            barrier, inc=1, device_id=(leaf, lax.rem(sib + o, n_sib)), device_id_type=MESH
        )
    for o in range(1, n_leaf):
        pl.semaphore_signal(
            barrier, inc=1, device_id=(lax.rem(leaf + o, n_leaf), sib), device_id_type=MESH
        )

    @pl.when(has_right)
    def _():
        pl.semaphore_signal(barrier, inc=1, device_id=right, device_id_type=MESH)

    @pl.when(has_left)
    def _():
        pl.semaphore_signal(barrier, inc=1, device_id=left, device_id_type=MESH)

    def halo(k, i):
        own = windows[k].at[leaf_dev + i]
        up = pltpu.make_async_remote_copy(
            src_ref=own, dst_ref=windows[k].at[i],
            send_sem=h_send.at[k, 0, i], recv_sem=h_recv.at[k, 0, i],
            device_id=right, device_id_type=MESH,
        )
        down = pltpu.make_async_remote_copy(
            src_ref=own, dst_ref=windows[k].at[2 * leaf_dev + i],
            send_sem=h_send.at[k, 1, i], recv_sem=h_recv.at[k, 1, i],
            device_id=left, device_id_type=MESH,
        )
        return up, down

    def send_block(k, i, value):
        windows[k][leaf_dev + i] = value.astype(jnp.bfloat16)
        up, down = halo(k, i)
        pl.when(has_right)(lambda: up.start())
        pl.when(has_left)(lambda: down.start())

    def wait_halo(k):
        @pl.when(has_left)
        def _():
            for i in range(leaf_dev):
                halo(k, i)[0].wait_recv()

        @pl.when(has_right)
        def _():
            for i in range(leaf_dev):
                halo(k, i)[1].wait_recv()

    def near_apply(k, i):
        total = None
        for m in range(near.shape[1]):
            t = jnp.clip(near[i, m] - (pos - 1) * leaf_dev, 0, 3 * leaf_dev - 1)
            part = jnp.dot(nearby[i, m], windows[k][t], preferred_element_type=jnp.float32)
            total = part if total is None else total + part
        return total

    def project(values):
        return sum(mm(lifted_t[:, blocks[i]], values[i]) for i in range(leaf_dev))

    def inverse_times(i, v):
        high, rest = split(v)
        wide = jnp.dot(
            d_high[i], jnp.concatenate([high, rest], axis=1), preferred_element_type=jnp.float32
        )
        small = jnp.dot(d_low[i], high, preferred_element_type=jnp.float32)
        return wide[:, : v.shape[1]] + (wide[:, v.shape[1] :] + small)

    core = jnp.zeros((rank, rank), jnp.float32)
    first = jnp.zeros((rank, columns), jnp.float32)
    row_ids = lax.broadcasted_iota(jnp.int32, (leaf_size, leaf_size), 0)
    loads[0].wait()
    loads[1].wait()
    for i, rows in enumerate(blocks):
        d_high[i], d_low[i] = split(diag[i])
        block = low[rows, :]
        up = mm(diag[i], block)
        lifted[rows, :] = up
        up_t = up.T
        lifted_t[:, rows] = up_t
        core += mm(up_t, block)
    sides = 1 - pos // last + (pos + last - 1) // last
    pl.semaphore_wait(barrier, n_sib + n_leaf - 2 + sides)
    for i, rows in enumerate(blocks):
        send_block(0, i, lifted[rows, :])
    loads[2].wait()
    loads[3].wait()
    scaled = []
    for i, rows in enumerate(blocks):
        local = order[i] - (pos * leaf_dev + i) * leaf_size
        pick = (row_ids == local).astype(jnp.float32).T.astype(jnp.bfloat16)
        value = src[rows, :]
        high = value.astype(jnp.bfloat16)
        value = value - high.astype(jnp.float32)
        parts = jnp.concatenate([high, *split(value)], axis=1)
        parts = jnp.dot(pick, parts, preferred_element_type=jnp.float32)
        ordered = parts[:, :columns] + (
            parts[:, columns : 2 * columns] + parts[:, 2 * columns :]
        )
        scaled.append(inverse_times(i, ordered))
        first += mm(lifted_t[:, rows], ordered)
    sums[0].src[0:rank, :] = core
    sums[0].src[rank:, :] = first

    sums[0].step()
    loads[4].wait()
    loads[5].wait()

    def power(j):
        wait_halo(j)
        image = []
        for i, rows in enumerate(blocks):
            image.append(near_apply(j, i))
            value = -inverse_times(i, image[i])
            powers[j, rows, :] = value
            if j + 1 < ITERS:
                send_block(j + 1, i, value)
        moment_sum.src[j * rank : (j + 1) * rank, :] = project(image)
        if j + 1 == ITERS:
            moment_sum.step()

    sums[0].step()
    sums[0].step()
    power(0)
    both = sums[0].result()
    eye = lax.broadcasted_iota(jnp.int32, (rank, rank), 0) == lax.broadcasted_iota(
        jnp.int32, (rank, rank), 1
    )
    core = both[:rank] + jnp.where(eye, 1.0, 0.0)
    first = both[rank:]
    base = ITERS
    start = guess(core, first)
    now = []
    for i, rows in enumerate(blocks):
        value = scaled[i] - mm(lifted[rows, :], start)
        send_block(base, i, value)
        x_first[rows, :] = value
        now.append(value)
    work[...] = core
    steps = list(range(0, rank, PIVOTS))
    share = len(steps) // ITERS

    power(1)
    eliminate(work, steps[:share])
    for k in range(ITERS):
        wait_halo(base + k)
        image, now = [], []
        for i, rows in enumerate(blocks):
            image.append(near_apply(base + k, i))
            now.append(x_first[rows, :] - inverse_times(i, image[i]))
            if k + 1 < ITERS:
                send_block(base + k + 1, i, now[i])
        target = early if k < 2 else late
        target.src[(k % 2) * rank : (k % 2 + 1) * rank, :] = project(image)
        if k == 3:
            late.step()
        if k >= 1:
            early.step()
        if k >= 2:
            moment_sum.step()
        if k + 2 < ITERS:
            power(k + 2)
        if k + 1 < ITERS:
            end = (k + 2) * share if k + 2 < ITERS else len(steps)
            eliminate(work, steps[(k + 1) * share : end])

    inverse = work[...]
    deltas = [mm(inverse, first) - start]
    spread = [mm(lifted[rows, :], inverse) for rows in blocks]
    shift = [mm(powers[0, rows, :], inverse) for rows in blocks]
    late.step()
    early.step()
    moment_sum.step()
    images = early.result()
    late.step()
    moments = moment_sum.result()
    moment = [moments[j * rank : (j + 1) * rank] for j in range(ITERS)]

    def solve(k):
        total = sum(mm(moment[j], deltas[k - 1 - j]) for j in range(k))
        if k <= 2:
            total -= images[(k - 1) * rank : k * rank]
        deltas.append(deltas[0] + mm(inverse, total))

    again = mm(moment[0], inverse)
    solve(1)
    solve(2)
    late.step()
    solve(3)
    solve(4)
    for i, rows in enumerate(blocks):
        value = now[i] - mm(lifted[rows, :], deltas[ITERS])
        for j in range(1, ITERS + 1):
            value -= mm(powers[j - 1, rows, :], deltas[ITERS - j])
        sol[rows, :] = value
        x_first[rows, :] = shift[i] + mm(spread[i], again)
        lifted[rows, :] = spread[i]
    coef[...] = start + deltas[ITERS]
    twice = mm(inverse, again)
    final = late.result()
    before, final = final[:rank], final[rank:]
    for rows in blocks:
        sol[rows, :] += mm(x_first[rows, :], before) + mm(lifted[rows, :], final)
    coef[...] -= mm(twice, before) + mm(inverse, final)

    for s in sums:
        s.sent()
    for k in range(2 * ITERS):
        for i in range(leaf_dev):
            up, down = halo(k, i)
            pl.when(has_right)(lambda up=up: up.wait_send())
            pl.when(has_left)(lambda down=down: down.wait_send())


def on_device(sources, ordering, diagonal_inverse, low_rank, nearby_blocks, near_index):
    n_leaf, n_sib = lax.axis_size("leaf"), lax.axis_size("sib")
    leaf_dev, leaf_size = diagonal_inverse.shape[:2]
    rows, columns = sources.shape
    rank = low_rank.shape[1]
    f32 = jnp.float32
    operands = (
        near_index,
        ordering.reshape(leaf_dev, 1, leaf_size),
        sources,
        diagonal_inverse,
        low_rank,
        nearby_blocks,
    )
    scratch = [pltpu.SMEM(near_index.shape, near_index.dtype)]
    scratch += [pltpu.VMEM(x.shape, x.dtype) for x in operands[1:]]
    scratch += [pltpu.SemaphoreType.DMA((len(operands),))]
    scratch += [
        pltpu.VMEM((3 * leaf_dev, leaf_size, columns), jnp.bfloat16) for _ in range(2 * ITERS)
    ]
    scratch += [
        pltpu.SemaphoreType.DMA((2 * ITERS, 2, leaf_dev)),
        pltpu.SemaphoreType.DMA((2 * ITERS, 2, leaf_dev)),
        pltpu.VMEM((rows, rank), f32),
        pltpu.VMEM((rank, rows), f32),
        pltpu.VMEM((ITERS, rows, rank), f32),
        pltpu.VMEM((rows, columns), f32),
        pltpu.VMEM((rank, rank), f32),
        pltpu.VMEM(diagonal_inverse.shape, jnp.bfloat16),
        pltpu.VMEM(diagonal_inverse.shape, jnp.bfloat16),
    ]
    for count in COUNTS:
        total = count * rank
        chunk = total // n_sib
        cut = parted(total, (n_leaf, n_sib))
        parts = n_leaf if cut else 1
        piece = chunk // parts
        scratch += [
            pltpu.VMEM((total, columns), f32),
            pltpu.VMEM((n_sib, chunk, columns), f32),
            pltpu.VMEM((parts, piece, columns), f32),
            pltpu.VMEM((n_leaf, piece, columns), f32),
            pltpu.VMEM((n_sib, parts, piece, columns), f32),
        ]
        scratch += [pltpu.SemaphoreType.DMA((4,)), pltpu.SemaphoreType.DMA((4,))]
    vmem = pl.BlockSpec(memory_space=pltpu.VMEM)
    return pl.pallas_call(
        functools.partial(kernel, (n_leaf, n_sib)),
        out_shape=(
            jax.ShapeDtypeStruct((rows, columns), f32),
            jax.ShapeDtypeStruct((rank, columns), f32),
        ),
        in_specs=[pl.BlockSpec(memory_space=pl.ANY)] * len(operands),
        out_specs=(vmem, vmem),
        scratch_shapes=scratch,
        compiler_params=pltpu.CompilerParams(
            collective_id=0, has_side_effects=True, vmem_limit_bytes=62 * 1024 * 1024
        ),
    )(*operands)


def solution(mesh):
    placed = (
        P(("leaf", "sib"), None),
        P(("leaf", "sib")),
        P(("leaf", "sib"), None, None),
        P(("leaf", "sib"), None),
        P(("leaf", "sib"), None, None, None),
        P(("leaf", "sib"), None),
    )
    return jax.shard_map(
        on_device,
        mesh=mesh,
        in_specs=placed,
        out_specs=(P(("leaf", "sib"), None), P()),
        check_vma=False,
    )
```

```python
import functools

import jax
import jax.numpy as jnp
from jax import lax
from jax.experimental import pallas as pl
from jax.experimental.pallas import tpu as pltpu
from jax.sharding import PartitionSpec as P

ITERS = 4
MESH = pl.DeviceIdType.MESH
HIGH = lax.Precision.HIGHEST
COUNTS = (2, ITERS, 2, 2)
PIVOTS = 16
LEVELS = 5


def mm(a, b):
    return jnp.dot(a, b, precision=HIGH, preferred_element_type=jnp.float32)


def mm_t(a, b):
    return lax.dot_general(
        a, b, (((0,), (0,)), ((), ())), precision=HIGH, preferred_element_type=jnp.float32
    )


def split(x):
    high = x.astype(jnp.bfloat16)
    return high, (x - high.astype(jnp.float32)).astype(jnp.bfloat16)


def guess(core, right):
    size = core.shape[0]
    eye = lax.broadcasted_iota(jnp.int32, (size, size), 0) == lax.broadcasted_iota(
        jnp.int32, (size, size), 1
    )
    bound = jnp.max(jnp.sum(jnp.abs(core), axis=1, keepdims=True), axis=0, keepdims=True)
    scale = 2.0 / (1.0 + bound)
    rest = jnp.where(eye, 1.0, 0.0) - core * scale
    value = right * scale
    for level in range(LEVELS):
        value += jnp.dot(rest, value, preferred_element_type=jnp.float32)
        if level + 1 < LEVELS:
            rest = jnp.dot(rest, rest, preferred_element_type=jnp.float32)
    return value


def split3(x):
    high = x.astype(jnp.bfloat16)
    return (high, *split(x - high.astype(jnp.float32)))


def eliminate(work, offsets):
    size = work.shape[0]
    lane = lax.broadcasted_iota(jnp.int32, (PIVOTS, size), 1)
    sub = lax.broadcasted_iota(jnp.int32, (PIVOTS, size), 0)
    wide = lax.broadcasted_iota(jnp.int32, (size, size), 1)
    for off in offsets:
        panel = work[off : off + PIVOTS, :]
        left = jnp.where(lane < off, -panel, panel)
        cols = [
            jnp.broadcast_to(panel[:, off + j : off + j + 1], panel.shape) for j in range(PIVOTS)
        ]
        inside = (lane >= off) & (lane < off + PIVOTS)
        panel = jnp.where(inside, jnp.where(lane == off + sub, 1.0, 0.0), panel)
        for j in range(PIVOTS):
            inv = 1.0 / cols[j][j : j + 1, :]
            row = panel[j : j + 1, :] * inv
            panel = jnp.where(sub == j, row, panel - cols[j] * row)
            for m in range(j + 1, PIVOTS):
                row = cols[m][j : j + 1, :] * inv
                cols[m] = jnp.where(sub == j, row, cols[m] - cols[j] * row)
        h, m, l = split3(left.T)
        rh, rm, rl = split3(panel)
        update = jnp.dot(
            jnp.concatenate([h, h, m, h, l, m], axis=1),
            jnp.concatenate([rh, rm, rh, rl, rh, rm], axis=0),
            preferred_element_type=jnp.float32,
        )
        inside = (wide >= off) & (wide < off + PIVOTS)
        work[...] = jnp.where(inside, 0.0, work[...]) - update
        work[off : off + PIVOTS, :] = panel


def parted(n, sizes):
    n_leaf, n_sib = sizes
    return (n // n_sib) % n_leaf == 0


class Sum:
    def __init__(self, me, sizes, refs):
        self.leaf, self.sib = me
        self.n_leaf, self.n_sib = sizes
        self.src, self.r1, self.t2, self.r2, self.r3, self.send, self.recv = refs
        self.chunk = self.r1.shape[1]
        self.parts, self.piece = self.r3.shape[1:3]
        self.open, self.now = [], None
        self.steps = [self.scatter_sib]
        if self.parts > 1:
            self.steps += [self.scatter_leaf, self.gather_leaf, self.gather_sib]
        else:
            self.steps += [self.exchange_leaf, self.gather_sib]

    def step(self):
        if self.steps:
            work, self.steps = self.steps[0], self.steps[1:]
            work()

    def arrived(self):
        phase, bulk = self.now
        pltpu.make_async_copy(bulk, bulk, self.recv.at[phase]).wait()

    def sent(self):
        for phase, bulk in self.open:
            pltpu.make_async_copy(bulk, bulk, self.send.at[phase]).wait()
        self.open = []

    def bulk(self, phase, ref):
        self.now = (phase, ref)
        self.open.append(self.now)

    def copy(self, src, dst, phase, target):
        pltpu.make_async_remote_copy(
            src_ref=src, dst_ref=dst, send_sem=self.send.at[phase], recv_sem=self.recv.at[phase],
            device_id=target, device_id_type=MESH,
        ).start()

    def sibs(self):
        for o in range(1, self.n_sib):
            to = lax.rem(self.sib + o, self.n_sib)
            yield o, to, (self.leaf, to)

    def leaves(self):
        for o in range(1, self.n_leaf):
            to = lax.rem(self.leaf + o, self.n_leaf)
            yield o, to, (to, self.sib)

    def scatter_sib(self):
        for o, to, place in self.sibs():
            rows = pl.ds(pl.multiple_of(to * self.chunk, 8), self.chunk)
            self.copy(self.src.at[rows], self.r1.at[o], 0, place)
        self.bulk(0, self.r1.at[1:])

    def own(self):
        rows = pl.ds(pl.multiple_of(self.sib * self.chunk, 8), self.chunk)
        total = self.src[rows, :]
        self.arrived()
        for o in range(1, self.n_sib):
            total += self.r1[o]
        return total

    def exchange_leaf(self):
        self.r2[self.leaf] = self.own()
        mine = self.r2.at[self.leaf]
        for o, to, place in self.leaves():
            self.copy(mine, mine, 1, place)
        self.bulk(1, self.r2.at[1:])

    def scatter_leaf(self):
        total = self.own()
        for o in range(self.n_leaf):
            self.t2[o] = total[o * self.piece : (o + 1) * self.piece]
        for o, to, place in self.leaves():
            self.copy(self.t2.at[to], self.r2.at[o], 1, place)
        self.bulk(1, self.r2.at[1:])

    def gather_leaf(self):
        self.arrived()
        total = self.t2[self.leaf]
        for o in range(1, self.n_leaf):
            total += self.r2[o]
        self.r3[self.sib, self.leaf] = total
        mine = self.r3.at[self.sib, self.leaf]
        for o, to, place in self.leaves():
            self.copy(mine, mine, 2, place)
        self.bulk(2, self.r3.at[0, 1:])

    def gather_sib(self):
        self.arrived()
        if self.parts == 1:
            total = self.r2[0]
            for o in range(1, self.n_leaf):
                total += self.r2[o]
            self.r3[self.sib, 0] = total
        mine = self.r3.at[self.sib]
        for o, to, place in self.sibs():
            self.copy(mine, mine, 3, place)
        self.bulk(3, self.r3.at[1:])

    def result(self):
        while self.steps:
            self.step()
        self.arrived()
        return jnp.concatenate(
            [self.r3[s, l] for s in range(self.n_sib) for l in range(self.parts)], axis=0
        )


def kernel(
    sizes, near_in, order_in, src_in, diag_in, low_in, nearby_in, sol, coef, *scratch
):
    n_leaf, n_sib = sizes
    leaf, sib = lax.axis_index("leaf"), lax.axis_index("sib")
    pos = leaf * n_sib + sib
    last = n_leaf * n_sib - 1
    (near, order, src, diag, low, nearby), in_sem, scratch = scratch[:6], scratch[6], scratch[7:]
    loads = [
        pltpu.make_async_copy(a, b, in_sem.at[i])
        for i, (a, b) in enumerate(
            ((low_in, low), (diag_in, diag), (order_in, order), (src_in, src),
             (near_in, near), (nearby_in, nearby))
        )
    ]
    for c in loads:
        c.start()
    leaf_dev, leaf_size = diag.shape[0], diag.shape[1]
    rank = low.shape[1]
    columns = src.shape[1]
    blocks = [slice(i * leaf_size, (i + 1) * leaf_size) for i in range(leaf_dev)]
    windows, scratch = scratch[: 2 * ITERS], scratch[2 * ITERS :]
    h_send, h_recv, lifted, lifted_t, powers, x_first, work, d_high, d_low = scratch[:9]
    scratch = scratch[9:]
    sums = [Sum((leaf, sib), sizes, scratch[7 * i : 7 * i + 7]) for i in range(len(COUNTS))]
    moment_sum, early, late = sums[1:]

    def place(p):
        return (p // n_sib, lax.rem(p, n_sib))

    right, left = place(jnp.minimum(pos + 1, last)), place(jnp.maximum(pos - 1, 0))
    has_right, has_left = pos < last, pos > 0

    barrier = pltpu.get_barrier_semaphore()
    for o in range(1, n_sib):
        pl.semaphore_signal(
            barrier, inc=1, device_id=(leaf, lax.rem(sib + o, n_sib)), device_id_type=MESH
        )
    for o in range(1, n_leaf):
        pl.semaphore_signal(
            barrier, inc=1, device_id=(lax.rem(leaf + o, n_leaf), sib), device_id_type=MESH
        )

    @pl.when(has_right)
    def _():
        pl.semaphore_signal(barrier, inc=1, device_id=right, device_id_type=MESH)

    @pl.when(has_left)
    def _():
        pl.semaphore_signal(barrier, inc=1, device_id=left, device_id_type=MESH)

    def halo(k, i):
        own = windows[k].at[leaf_dev + i]
        up = pltpu.make_async_remote_copy(
            src_ref=own, dst_ref=windows[k].at[i],
            send_sem=h_send.at[k, 0, i], recv_sem=h_recv.at[k, 0, i],
            device_id=right, device_id_type=MESH,
        )
        down = pltpu.make_async_remote_copy(
            src_ref=own, dst_ref=windows[k].at[2 * leaf_dev + i],
            send_sem=h_send.at[k, 1, i], recv_sem=h_recv.at[k, 1, i],
            device_id=left, device_id_type=MESH,
        )
        return up, down

    def send_block(k, i, value):
        windows[k][leaf_dev + i] = value.astype(jnp.bfloat16)
        up, down = halo(k, i)
        pl.when(has_right)(lambda: up.start())
        pl.when(has_left)(lambda: down.start())

    def wait_halo(k):
        @pl.when(has_left)
        def _():
            for i in range(leaf_dev):
                halo(k, i)[0].wait_recv()

        @pl.when(has_right)
        def _():
            for i in range(leaf_dev):
                halo(k, i)[1].wait_recv()

    def near_apply(k, i):
        total = None
        for m in range(near.shape[1]):
            t = jnp.clip(near[i, m] - (pos - 1) * leaf_dev, 0, 3 * leaf_dev - 1)
            part = jnp.dot(nearby[i, m], windows[k][t], preferred_element_type=jnp.float32)
            total = part if total is None else total + part
        return total

    def project(values):
        total = 0.0
        for rows, v in zip(blocks, values):
            high, rest = split(v)
            left, left_rest = split(lifted_t[:, rows])
            wide = jnp.dot(
                left, jnp.concatenate([high, rest], axis=1), preferred_element_type=jnp.float32
            )
            small = jnp.dot(left_rest, high, preferred_element_type=jnp.float32)
            total += wide[:, :columns] + (wide[:, columns:] + small)
        return total

    def inverse_times(i, v):
        high, rest = split(v)
        wide = jnp.dot(
            d_high[i], jnp.concatenate([high, rest], axis=1), preferred_element_type=jnp.float32
        )
        small = jnp.dot(d_low[i], high, preferred_element_type=jnp.float32)
        return wide[:, : v.shape[1]] + (wide[:, v.shape[1] :] + small)

    core = jnp.zeros((rank, rank), jnp.float32)
    first = jnp.zeros((rank, columns), jnp.float32)
    row_ids = lax.broadcasted_iota(jnp.int32, (leaf_size, leaf_size), 0)
    loads[0].wait()
    loads[1].wait()
    for i, rows in enumerate(blocks):
        d_high[i], d_low[i] = split(diag[i])
        block = low[rows, :]
        up = mm(diag[i], block)
        lifted[rows, :] = up
        up_t = up.T
        lifted_t[:, rows] = up_t
        core += mm(up_t, block)
    sides = 1 - pos // last + (pos + last - 1) // last
    pl.semaphore_wait(barrier, n_sib + n_leaf - 2 + sides)
    for i, rows in enumerate(blocks):
        send_block(0, i, lifted[rows, :])
    loads[2].wait()
    loads[3].wait()
    scaled = []
    for i, rows in enumerate(blocks):
        local = order[i] - (pos * leaf_dev + i) * leaf_size
        pick = (row_ids == local).astype(jnp.float32).T.astype(jnp.bfloat16)
        value = src[rows, :]
        high = value.astype(jnp.bfloat16)
        value = value - high.astype(jnp.float32)
        parts = jnp.concatenate([high, *split(value)], axis=1)
        parts = jnp.dot(pick, parts, preferred_element_type=jnp.float32)
        ordered = parts[:, :columns] + (
            parts[:, columns : 2 * columns] + parts[:, 2 * columns :]
        )
        scaled.append(inverse_times(i, ordered))
        first += mm(lifted_t[:, rows], ordered)
    sums[0].src[0:rank, :] = core
    sums[0].src[rank:, :] = first

    sums[0].step()
    loads[4].wait()
    loads[5].wait()

    def power(j):
        wait_halo(j)
        image = []
        for i, rows in enumerate(blocks):
            image.append(near_apply(j, i))
            value = -inverse_times(i, image[i])
            powers[j, rows, :] = value
            if j + 1 < ITERS:
                send_block(j + 1, i, value)
        moment_sum.src[j * rank : (j + 1) * rank, :] = project(image)
        if j + 1 == ITERS:
            moment_sum.step()

    sums[0].step()
    sums[0].step()
    power(0)
    both = sums[0].result()
    eye = lax.broadcasted_iota(jnp.int32, (rank, rank), 0) == lax.broadcasted_iota(
        jnp.int32, (rank, rank), 1
    )
    core = both[:rank] + jnp.where(eye, 1.0, 0.0)
    first = both[rank:]
    base = ITERS
    start = guess(core, first)
    now = []
    for i, rows in enumerate(blocks):
        value = scaled[i] - mm(lifted[rows, :], start)
        send_block(base, i, value)
        x_first[rows, :] = value
        now.append(value)
    work[...] = core
    steps = list(range(0, rank, PIVOTS))
    share = len(steps) // ITERS

    power(1)
    eliminate(work, steps[:share])
    for k in range(ITERS):
        wait_halo(base + k)
        image, now = [], []
        for i, rows in enumerate(blocks):
            image.append(near_apply(base + k, i))
            now.append(x_first[rows, :] - inverse_times(i, image[i]))
            if k + 1 < ITERS:
                send_block(base + k + 1, i, now[i])
        target = early if k < 2 else late
        target.src[(k % 2) * rank : (k % 2 + 1) * rank, :] = project(image)
        if k == 3:
            late.step()
        if k >= 1:
            early.step()
        if k >= 2:
            moment_sum.step()
        if k + 2 < ITERS:
            power(k + 2)
        if k + 1 < ITERS:
            end = (k + 2) * share if k + 2 < ITERS else len(steps)
            eliminate(work, steps[(k + 1) * share : end])

    inverse = work[...]
    deltas = [mm(inverse, first) - start]
    spread = [mm(lifted[rows, :], inverse) for rows in blocks]
    shift = [mm(powers[0, rows, :], inverse) for rows in blocks]
    late.step()
    early.step()
    moment_sum.step()
    images = early.result()
    late.step()
    moments = moment_sum.result()
    moment = [moments[j * rank : (j + 1) * rank] for j in range(ITERS)]

    def solve(k):
        total = sum(mm(moment[j], deltas[k - 1 - j]) for j in range(k))
        if k <= 2:
            total -= images[(k - 1) * rank : k * rank]
        deltas.append(deltas[0] + mm(inverse, total))

    again = mm(moment[0], inverse)
    solve(1)
    solve(2)
    late.step()
    solve(3)
    solve(4)
    for i, rows in enumerate(blocks):
        value = now[i] - mm(lifted[rows, :], deltas[ITERS])
        for j in range(1, ITERS + 1):
            value -= mm(powers[j - 1, rows, :], deltas[ITERS - j])
        sol[rows, :] = value
        x_first[rows, :] = shift[i] + mm(spread[i], again)
        lifted[rows, :] = spread[i]
    coef[...] = start + deltas[ITERS]
    twice = mm(inverse, again)
    final = late.result()
    before, final = final[:rank], final[rank:]
    for rows in blocks:
        sol[rows, :] += mm(x_first[rows, :], before) + mm(lifted[rows, :], final)
    coef[...] -= mm(twice, before) + mm(inverse, final)

    for s in sums:
        s.sent()
    for k in range(2 * ITERS):
        for i in range(leaf_dev):
            up, down = halo(k, i)
            pl.when(has_right)(lambda up=up: up.wait_send())
            pl.when(has_left)(lambda down=down: down.wait_send())


def on_device(sources, ordering, diagonal_inverse, low_rank, nearby_blocks, near_index):
    n_leaf, n_sib = lax.axis_size("leaf"), lax.axis_size("sib")
    leaf_dev, leaf_size = diagonal_inverse.shape[:2]
    rows, columns = sources.shape
    rank = low_rank.shape[1]
    f32 = jnp.float32
    operands = (
        near_index,
        ordering.reshape(leaf_dev, 1, leaf_size),
        sources,
        diagonal_inverse,
        low_rank,
        nearby_blocks,
    )
    scratch = [pltpu.SMEM(near_index.shape, near_index.dtype)]
    scratch += [pltpu.VMEM(x.shape, x.dtype) for x in operands[1:]]
    scratch += [pltpu.SemaphoreType.DMA((len(operands),))]
    scratch += [
        pltpu.VMEM((3 * leaf_dev, leaf_size, columns), jnp.bfloat16) for _ in range(2 * ITERS)
    ]
    scratch += [
        pltpu.SemaphoreType.DMA((2 * ITERS, 2, leaf_dev)),
        pltpu.SemaphoreType.DMA((2 * ITERS, 2, leaf_dev)),
        pltpu.VMEM((rows, rank), f32),
        pltpu.VMEM((rank, rows), f32),
        pltpu.VMEM((ITERS, rows, rank), f32),
        pltpu.VMEM((rows, columns), f32),
        pltpu.VMEM((rank, rank), f32),
        pltpu.VMEM(diagonal_inverse.shape, jnp.bfloat16),
        pltpu.VMEM(diagonal_inverse.shape, jnp.bfloat16),
    ]
    for count in COUNTS:
        total = count * rank
        chunk = total // n_sib
        cut = parted(total, (n_leaf, n_sib))
        parts = n_leaf if cut else 1
        piece = chunk // parts
        scratch += [
            pltpu.VMEM((total, columns), f32),
            pltpu.VMEM((n_sib, chunk, columns), f32),
            pltpu.VMEM((parts, piece, columns), f32),
            pltpu.VMEM((n_leaf, piece, columns), f32),
            pltpu.VMEM((n_sib, parts, piece, columns), f32),
        ]
        scratch += [pltpu.SemaphoreType.DMA((4,)), pltpu.SemaphoreType.DMA((4,))]
    vmem = pl.BlockSpec(memory_space=pltpu.VMEM)
    return pl.pallas_call(
        functools.partial(kernel, (n_leaf, n_sib)),
        out_shape=(
            jax.ShapeDtypeStruct((rows, columns), f32),
            jax.ShapeDtypeStruct((rank, columns), f32),
        ),
        in_specs=[pl.BlockSpec(memory_space=pl.ANY)] * len(operands),
        out_specs=(vmem, vmem),
        scratch_shapes=scratch,
        compiler_params=pltpu.CompilerParams(
            collective_id=0, has_side_effects=True, vmem_limit_bytes=62 * 1024 * 1024
        ),
    )(*operands)


def solution(mesh):
    placed = (
        P(("leaf", "sib"), None),
        P(("leaf", "sib")),
        P(("leaf", "sib"), None, None),
        P(("leaf", "sib"), None),
        P(("leaf", "sib"), None, None, None),
        P(("leaf", "sib"), None),
    )
    return jax.shard_map(
        on_device,
        mesh=mesh,
        in_specs=placed,
        out_specs=(P(("leaf", "sib"), None), P()),
        check_vma=False,
    )
```
